128 devices in a mesh: seq: 16 (over y, x), head: 8 (over z, core).
Axes of the slice: x: 4, y: 4, z: 4, core: 2. Of those that a mesh axis runs over, the one named last changes fastest.
Arguments:
- queries: bfloat16 [32768, 2048], P(('seq', 'head')), may hold values from -8 to 8
- keys: bfloat16 [32768, 2048], P(('seq', 'head')), may hold values from -8 to 8
- values: bfloat16 [32768, 2048], P(('seq', 'head')), may hold values from -6 to 6
- lengths: int32 [16, 3], replicated, may hold values from 1 to 10, 16 in all within a row
- plan: int32 [256], replicated, may hold values from 0 to 255, as said below
Outputs:
- attended: bfloat16 [32768, 2048], P(('seq', 'head'))
The draws below stay inside these ranges and needn't reach their ends.
Inputs may be any that keep to these rules, and one draw needn't show every extreme that they name: `lengths`: each row sums to 16. A permutation of the block indices. Stream block b lies in group b // 16 and goes to group plan[b] // 16; each group sends exactly 2 blocks to each of 8 distinct groups, among them itself, the next group (index + 1, counted round) and the group 16 // 2 away (index + 8, counted round), and none to any other, and the 2 blocks of one device go to distinct groups.
All inputs are finite; a program needn't handle non-finite values.
Results may differ from the reference program's by a relative error of at most 0.0047.
Values may be sent and summed in bfloat16 or wider, within the bound.
A program may use at most 128 MiB of HBM per device.

```python
import math
import jax
import jax.numpy as jnp
import numpy as np
from jax import lax

HEADS = 16
HEAD_DIM = 128
BLOCK = 128
RECS = 3
FEATURES = 2048
GROUPS = 16
GROUP_ROWS = 2048
BPG = 16
CAP = 2
LONGEST = 10
NBLOCKS = 256
TOKENS = 32768


def draw_queries(key, part):
    key = jax.random.fold_in(key, 5)
    base = jax.random.truncated_normal(key, -6.0, 6.0, (TOKENS, FEATURES))
    return base.astype(jnp.bfloat16)


def draw_keys(key, part):
    key = jax.random.fold_in(key, 7)
    base = jax.random.truncated_normal(key, -6.0, 6.0, (TOKENS, FEATURES))
    return base.astype(jnp.bfloat16)


def draw_plan(key, part):
    key = jax.random.fold_in(key, 11)
    key_offset, key_slots, key_turn = jax.random.split(key, 3)
    classes_count = BPG // CAP
    halfway = GROUPS // 2
    drawn = 2 + jax.random.permutation(key_offset, GROUPS - 3).astype(jnp.int32)
    others = jnp.where(drawn >= halfway, drawn + 1, drawn).astype(jnp.int32)
    offsets = jnp.concatenate([jnp.array([0, 1, halfway], dtype=jnp.int32), others])[:classes_count]
    slot_keys = jax.random.split(key_slots, GROUPS)
    slot_perm = jax.vmap(lambda one: jax.random.permutation(one, BPG))(slot_keys).astype(jnp.int32)
    rotation = jax.random.randint(key_turn, (GROUPS, 1), 0, classes_count).astype(jnp.int32)
    source = jnp.arange(GROUPS, dtype=jnp.int32)[:, None]
    block_ids = jnp.arange(BPG, dtype=jnp.int32)[None, :]
    klass = (block_ids + rotation) % classes_count
    turn = block_ids // classes_count
    target = (source + offsets[klass]) % GROUPS
    raw_slot = klass * CAP + turn
    slot = slot_perm[target, raw_slot]
    return (target * BPG + slot).reshape(NBLOCKS).astype(jnp.int32)


def levels(key, dims, cuts, low, largest):
    gain, own = 1.0, jax.random.fold_in(key, 6)
    for axis_at, blocks in cuts:
        draws = jnp.exp(jax.random.uniform(jax.random.fold_in(own, axis_at), (blocks,), jnp.float32, low / len(cuts), largest / len(cuts)))
        gain = gain * jnp.repeat(draws, dims[axis_at] // blocks).reshape([-1 if axis == axis_at else 1 for axis in range(len(dims))])
    return gain


def length_profile(amount, total, reach, skew):
    weights = [(1 << 20) // math.isqrt(rank ** skew) + 1 for rank in range(2, amount + 1)]
    surplus, given = total - reach - (amount - 1), [1] * (amount - 1)
    while surplus > 0:
        free = [i for i in range(amount - 1) if given[i] < reach]
        whole, budget = sum([weights[i] for i in free]), surplus
        for i in free:
            addition = min(reach - given[i], max(1, budget * weights[i] // whole), surplus)
            given[i] = given[i] + addition
            surplus = surplus - addition
    return np.array([reach] + given)


def uneven_parts(own_key, count, total, limit, lean):
    if count == 2:
        one = jax.random.randint(own_key, (), max(1, total - limit), min(limit, total - 1) + 1)
        return jnp.stack([one, total - one])
    tallies = jnp.asarray(length_profile(count, total, limit, lean), jnp.int32)
    couples = (count - 1) // 2
    giver, sink = tallies[1:1 + 2 * couples:2], tallies[2:2 + 2 * couples:2]
    room = jnp.minimum(giver - 1, limit - sink)
    shifted = jax.random.randint(jax.random.fold_in(own_key, 1), (couples,), 0, 1 << 20) % (room + 1)
    tallies = tallies.at[1:1 + 2 * couples:2].set(giver - shifted).at[2:2 + 2 * couples:2].set(sink + shifted)
    return tallies[jax.random.permutation(jax.random.fold_in(own_key, 2), count)]


def gaussian(own_key, dims, width, reach, cuts=(), held_as=jnp.bfloat16):
    factor_of = levels(own_key, dims, cuts, -0.22, 0.18) if cuts else 1.0
    entries = jax.random.normal(own_key, dims, jnp.float32) * width * factor_of
    return jnp.minimum(jnp.maximum(entries, -reach), reach).astype(held_as)


def setup_inputs(seed: int = 0) -> dict:
    key_of = jax.random.split(jax.random.key(seed), 6)
    queries = draw_queries(jax.random.fold_in(key_of[5], 71), 0)
    keys = draw_keys(jax.random.fold_in(key_of[5], 71), 0)
    values = gaussian(key_of[2], (TOKENS, FEATURES), 1.0, 6.0, ((0, 128),))
    lengths = jax.vmap(lambda own: uneven_parts(own, RECS, BPG, LONGEST, 2))(jax.random.split(key_of[3], GROUPS)).reshape((GROUPS, RECS)).astype(jnp.int32)
    plan = draw_plan(jax.random.fold_in(key_of[5], 71), 0)
    return {"queries": queries, "keys": keys, "values": values, "lengths": lengths, "plan": plan}


def group_attention(item):
    q_rows, k_rows, v_rows, lens = item
    total = GROUP_ROWS
    ends = (jnp.cumsum(lens) * BLOCK).astype(jnp.int32)
    positions = jnp.arange(total, dtype=jnp.int32)
    record = lax.optimization_barrier(jnp.sum((positions[:, None] >= ends[None, :]).astype(jnp.int32), axis=1))
    factor = 1.0 / math.sqrt(HEAD_DIM)
    span = min(512, total)
    pieces = []
    for start in range(0, total, span):
        stop = start + span
        q_part = q_rows[start:stop].astype(jnp.float32)
        k_part = k_rows[:stop].astype(jnp.float32)
        v_part = v_rows[:stop].astype(jnp.float32)
        scores = jnp.einsum('qhd,khd->hqk', q_part, k_part) * factor
        visible = (record[start:stop, None] == record[None, :stop]) & (positions[None, :stop] <= positions[start:stop, None])
        scores = jnp.where(visible[None], scores, -1e+30)
        peak = lax.optimization_barrier(jnp.max(scores, axis=-1, keepdims=True))
        expo = jnp.exp(scores - peak)
        weights = (expo / lax.optimization_barrier(jnp.sum(expo, axis=-1, keepdims=True))).astype(jnp.bfloat16)
        output = jnp.einsum('hqk,khd->qhd', weights.astype(jnp.float32), v_part)
        pieces.append(output.astype(jnp.bfloat16))
    return jnp.concatenate(pieces, axis=0)

def reference(queries, keys, values, lengths, plan):

    def regroup(array):
        blocks = array.reshape(NBLOCKS, BLOCK, FEATURES)
        placed = jnp.zeros_like(blocks).at[plan].set(blocks)
        return placed.reshape(GROUPS, GROUP_ROWS, HEADS, HEAD_DIM)
    balanced = lax.map(group_attention, (regroup(queries), regroup(keys), regroup(values), lengths))
    blocks = balanced.reshape(NBLOCKS, BLOCK, FEATURES)
    return blocks[plan].reshape(TOKENS, FEATURES)
```

```python
import functools
import math

import jax
import jax.numpy as jnp
from jax import lax
from jax.experimental import pallas as pl
from jax.experimental.pallas import tpu as pltpu
from jax.sharding import PartitionSpec as P

HEAD_DIM = 128
BLOCK = 128
SIDE = 4
SEQ = 16
HEAD = 8
BPG = 16
CAP = 2
LONGEST = 10
HEADS_HERE = 2
PAD = LONGEST - 1
WINDOW = LONGEST * BLOCK
MESH = pl.DeviceIdType.MESH
SCALE = 1.0 / math.sqrt(HEAD_DIM)
LOG2E = 1.4426950408889634

ORDER = (
    (1, 0), (0, 1), (3, 0), (0, 3), (2, 0), (0, 2), (1, 1), (3, 3),
    (1, 3), (3, 1), (2, 1), (1, 2), (2, 3), (3, 2), (2, 2),
)
CHUNKS = ((1, 0), (0, 0), (2, 0), (1, 1), (0, 1), (2, 1))
PACK, PLACE, REPACK, RETURN = 0, 32, 48, 80


def tables(plan, group):
    grid = plan.reshape(SEQ, BPG)
    dest, slot = grid // BPG, grid % BPG
    ids = jnp.arange(BPG, dtype=jnp.int32)
    same = (dest[:, :, None] == dest[:, None, :]) & (ids[None, None, :] < ids[None, :, None])
    rank = jnp.sum(same.astype(jnp.int32), axis=2)
    source = jnp.arange(SEQ, dtype=jnp.int32)[:, None]
    offset = ((dest // SIDE - source // SIDE) % SIDE) * SIDE + (dest % SIDE - source % SIDE) % SIDE
    cell = offset * CAP + rank
    cells = jnp.arange(SEQ * CAP, dtype=jnp.int32)
    my_cell = lax.dynamic_index_in_dim(cell, group, 0, keepdims=False)
    pack = jnp.sum(jnp.where(my_cell[None, :] == cells[:, None], ids[None, :], 0), axis=1)
    here = (dest == group).reshape(1, -1)
    flat_cell, flat_slot = cell.reshape(1, -1), slot.reshape(1, -1)
    place = jnp.sum(jnp.where(here & (flat_slot == ids[:, None]), flat_cell, 0), axis=1)
    repack = jnp.sum(jnp.where(here & (flat_cell == cells[:, None]), flat_slot, 0), axis=1)
    return jnp.concatenate([pack, place, repack, my_cell]).astype(jnp.int32)


def kernel(table, lengths, q_in, k_in, v_in, out, *scratch):
    zbuf, xbuf = scratch[0:6], scratch[6:12]
    pbuf, obuf, rbuf = scratch[12], scratch[13:15], scratch[15:17]
    opack, zpack, qg, kg, vg = scratch[17:22]
    z_send, z_recv, z_own, x_send, x_recv, y_send, y_recv, w_send, w_recv, w_own = scratch[22:]
    inputs = (q_in, k_in, v_in)
    s = lax.axis_index("seq")
    h = lax.axis_index("head")
    y, x = s // SIDE, s % SIDE

    def across(dx, dy):
        return (((y + dy) % SIDE) * SIDE + (x + dx) % SIDE, h)

    def peer(step):
        return lax.rem(h + step, HEAD)

    barrier = pltpu.get_barrier_semaphore()
    for dx, dy in ORDER:
        pl.semaphore_signal(barrier, inc=1, device_id=across(dx, dy), device_id_type=MESH)
    for step in range(1, HEAD):
        pl.semaphore_signal(barrier, inc=1, device_id=(s, peer(step)), device_id_type=MESH)
    pl.semaphore_wait(barrier, len(ORDER) + HEAD - 1)

    def z_copy(c, step):
        tensor, head = CHUNKS[c]
        to = peer(step)
        column = pl.multiple_of((to * HEADS_HERE + head) * HEAD_DIM, HEAD_DIM)
        return pltpu.make_async_remote_copy(
            src_ref=inputs[tensor].at[:, :, pl.ds(column, HEAD_DIM)],
            dst_ref=zbuf[c].at[pl.ds(h * CAP, CAP)],
            send_sem=z_send.at[c, step],
            recv_sem=z_recv.at[c, step],
            device_id=(s, to),
            device_id_type=MESH,
        )

    def z_local(c):
        tensor, head = CHUNKS[c]
        column = pl.multiple_of((h * HEADS_HERE + head) * HEAD_DIM, HEAD_DIM)
        return pltpu.make_async_copy(
            inputs[tensor].at[:, :, pl.ds(column, HEAD_DIM)],
            zbuf[c].at[pl.ds(h * CAP, CAP)],
            z_own.at[c],
        )

    def z_start(c):
        for step in range(1, HEAD):
            z_copy(c, step).start()
        z_local(c).start()

    def z_wait(c):
        z_local(c).wait()
        for step in range(1, HEAD):
            z_copy(c, step).wait_recv()

    def x_copy(c, dx, dy):
        offset = dy * SIDE + dx
        return pltpu.make_async_remote_copy(
            src_ref=pbuf.at[c, offset],
            dst_ref=xbuf[c].at[pl.ds(offset * CAP, CAP)],
            send_sem=x_send.at[c, offset],
            recv_sem=x_recv.at[c, offset],
            device_id=across(dx, dy),
            device_id_type=MESH,
        )

    def rows_of(index):
        return pl.ds(pl.multiple_of(index * BLOCK, BLOCK), BLOCK)

    def x_start(c):
        for dx, dy in ORDER:
            offset = dy * SIDE + dx
            for j in range(CAP):
                pbuf[c, offset, j] = zbuf[c][table[PACK + offset * CAP + j]]
            x_copy(c, dx, dy).start()
        for j in range(CAP):
            xbuf[c][j] = zbuf[c][table[PACK + j]]

    def x_wait(c):
        for dx, dy in ORDER:
            x_copy(c, dx, dy).wait_recv()

    first_end = lengths[s, 0]
    second_end = first_end + lengths[s, 1]

    def attend(head):
        k_chunk, q_chunk, v_chunk = (xbuf[3 * head + i] for i in range(3))

        def gather(r, carry):
            index = table[PLACE + r]
            rows, padded = rows_of(r), rows_of(r + PAD)
            qg[rows] = q_chunk[index]
            kg[padded] = k_chunk[index]
            vg[padded, :HEAD_DIM] = v_chunk[index]
            return carry

        lax.fori_loop(0, BPG, gather, 0)
        behind = lax.broadcasted_iota(jnp.int32, (1, WINDOW), 1) // BLOCK - PAD

        def record(index):
            return (index >= first_end).astype(jnp.int32) + (index >= second_end).astype(jnp.int32)

        down = lax.broadcasted_iota(jnp.int32, (BLOCK, BLOCK), 0)
        along = lax.broadcasted_iota(jnp.int32, (BLOCK, BLOCK), 1)
        corner = jnp.where(along <= down, 0.0, -1e30).astype(jnp.float32)

        def block(i, carry):
            theirs = behind + i
            seen = (record(theirs) == record(jnp.full_like(theirs, i))) & (theirs >= 0)
            bias = jnp.where(seen, 0.0, -1e30).astype(jnp.float32)
            window = pl.ds(pl.multiple_of(i * BLOCK, BLOCK), WINDOW)
            scores = lax.dot_general(
                qg[rows_of(i)], kg[window], (((1,), (1,)), ((), ())), preferred_element_type=jnp.float32
            )
            scores = jnp.concatenate(
                [scores[:, : WINDOW - BLOCK] + bias[:, : WINDOW - BLOCK], scores[:, WINDOW - BLOCK :] + corner], axis=1
            )
            peak = jnp.max(scores, axis=1, keepdims=True)
            weights = jnp.exp2((scores - peak) * (SCALE * LOG2E)).astype(jnp.bfloat16)
            both = jnp.dot(weights, vg[window], preferred_element_type=jnp.float32)
            obuf[head][i] = (both[:, :HEAD_DIM] / both[:, HEAD_DIM:]).astype(jnp.bfloat16)
            return carry

        lax.fori_loop(0, BPG, block, 0)

    def y_copy(head, dx, dy):
        offset = dy * SIDE + dx
        return pltpu.make_async_remote_copy(
            src_ref=opack.at[head, offset],
            dst_ref=rbuf[head].at[pl.ds(offset * CAP, CAP)],
            send_sem=y_send.at[head, offset],
            recv_sem=y_recv.at[head, offset],
            device_id=across(SIDE - dx, SIDE - dy),
            device_id_type=MESH,
        )

    def y_start(head):
        for dx, dy in ORDER:
            offset = dy * SIDE + dx
            for j in range(CAP):
                opack[head, offset, j] = obuf[head][table[REPACK + offset * CAP + j]]
            y_copy(head, dx, dy).start()
        for j in range(CAP):
            rbuf[head][j] = obuf[head][table[REPACK + j]]

    def w_copy(head, step):
        to = peer(step)
        column = pl.multiple_of((h * HEADS_HERE + head) * HEAD_DIM, HEAD_DIM)
        return pltpu.make_async_remote_copy(
            src_ref=zpack.at[head, to],
            dst_ref=out.at[:, :, pl.ds(column, HEAD_DIM)],
            send_sem=w_send.at[head, step],
            recv_sem=w_recv.at[head, step],
            device_id=(s, to),
            device_id_type=MESH,
        )

    def w_local(head):
        column = pl.multiple_of((h * HEADS_HERE + head) * HEAD_DIM, HEAD_DIM)
        return pltpu.make_async_copy(
            zpack.at[head, h], out.at[:, :, pl.ds(column, HEAD_DIM)], w_own.at[head]
        )

    def w_start(head):
        for dx, dy in ORDER:
            y_copy(head, dx, dy).wait_recv()
        for step in range(1, HEAD + 1):
            to = peer(step)
            for j in range(CAP):
                zpack[head, to, j] = rbuf[head][table[RETURN + to * CAP + j]]
            if step < HEAD:
                w_copy(head, step).start()
            else:
                w_local(head).start()

    z_start(0)
    z_start(1)
    kg[: PAD * BLOCK] = jnp.zeros((PAD * BLOCK, HEAD_DIM), jnp.bfloat16)
    vg[: PAD * BLOCK, :HEAD_DIM] = jnp.zeros((PAD * BLOCK, HEAD_DIM), jnp.bfloat16)
    vg[:, HEAD_DIM:] = jnp.ones(((PAD + BPG) * BLOCK, HEAD_DIM), jnp.bfloat16)
    for c in range(6):
        z_wait(c)
        x_start(c)
        if c + 2 < 6:
            z_start(c + 2)
    for head in range(HEADS_HERE):
        for c in range(3 * head, 3 * head + 3):
            x_wait(c)
        attend(head)
        y_start(head)
    for head in range(HEADS_HERE):
        w_start(head)
    for head in range(HEADS_HERE):
        w_local(head).wait()
        for step in range(1, HEAD):
            w_copy(head, step).wait()
        for dx, dy in ORDER:
            y_copy(head, dx, dy).wait_send()
    for c in range(6):
        for step in range(1, HEAD):
            z_copy(c, step).wait_send()
        for dx, dy in ORDER:
            x_copy(c, dx, dy).wait_send()


def local(queries, keys, values, lengths, plan):
    table = tables(plan, lax.axis_index("seq"))
    queries, keys, values = (array.reshape(CAP, BLOCK, -1) for array in (queries, keys, values))
    bf16 = jnp.bfloat16
    attended = pl.pallas_call(
        kernel,
        out_shape=jax.ShapeDtypeStruct(queries.shape, bf16),
        in_specs=[pl.BlockSpec(memory_space=pltpu.SMEM)] * 2 + [pl.BlockSpec(memory_space=pl.ANY)] * 3,
        out_specs=pl.BlockSpec(memory_space=pl.ANY),
        scratch_shapes=[pltpu.VMEM((BPG, BLOCK, HEAD_DIM), bf16)] * 6
        + [pltpu.VMEM((SEQ * CAP, BLOCK, HEAD_DIM), bf16)] * 6
        + [pltpu.VMEM((6, SEQ, CAP, BLOCK, HEAD_DIM), bf16)]
        + [pltpu.VMEM((BPG, BLOCK, HEAD_DIM), bf16)] * 2
        + [pltpu.VMEM((SEQ * CAP, BLOCK, HEAD_DIM), bf16)] * 2
        + [
            pltpu.VMEM((HEADS_HERE, SEQ, CAP, BLOCK, HEAD_DIM), bf16),
            pltpu.VMEM((HEADS_HERE, HEAD, CAP, BLOCK, HEAD_DIM), bf16),
            pltpu.VMEM((BPG * BLOCK, HEAD_DIM), bf16),
            pltpu.VMEM(((PAD + BPG) * BLOCK, HEAD_DIM), bf16),
            pltpu.VMEM(((PAD + BPG) * BLOCK, 2 * HEAD_DIM), bf16),
            pltpu.SemaphoreType.DMA((6, HEAD)),
            pltpu.SemaphoreType.DMA((6, HEAD)),
            pltpu.SemaphoreType.DMA((6,)),
            pltpu.SemaphoreType.DMA((6, SEQ)),
            pltpu.SemaphoreType.DMA((6, SEQ)),
            pltpu.SemaphoreType.DMA((HEADS_HERE, SEQ)),
            pltpu.SemaphoreType.DMA((HEADS_HERE, SEQ)),
            pltpu.SemaphoreType.DMA((HEADS_HERE, HEAD)),
            pltpu.SemaphoreType.DMA((HEADS_HERE, HEAD)),
            pltpu.SemaphoreType.DMA((HEADS_HERE,)),
        ],
        compiler_params=pltpu.CompilerParams(
            collective_id=0, has_side_effects=True, vmem_limit_bytes=44 * 2**20
        ),
        cost_estimate=pl.CostEstimate(flops=2_000_000_000, bytes_accessed=4 * 2**20, transcendentals=4_000_000),
    )(table, lengths, queries, keys, values)
    return attended.reshape(CAP * BLOCK, -1)


def solution(mesh):
    placed = (
        P(("seq", "head"), None),
        P(("seq", "head"), None),
        P(("seq", "head"), None),
        P(),
        P(),
    )
    return jax.shard_map(
        local, mesh=mesh, in_specs=placed, out_specs=P(("seq", "head"), None), check_vma=False
    )
```

```python
import functools
import math

import jax
import jax.numpy as jnp
from jax import lax
from jax.experimental import pallas as pl
from jax.experimental.pallas import tpu as pltpu
from jax.sharding import PartitionSpec as P

HEAD_DIM = 128
BLOCK = 128
SEQ = 16
HEAD = 8
BPG = 16
CAP = 2
LONGEST = 10
HEADS_HERE = 2
PAD = LONGEST - 1
WINDOW = LONGEST * BLOCK
MESH = pl.DeviceIdType.MESH
SCALE = 1.0 / math.sqrt(HEAD_DIM)
LOG2E = 1.4426950408889634
QUERY, KEY, VALUE = 0, 1, 2

COMING = (
    (KEY, 0, 0, 64), (KEY, 0, 64, 64), (QUERY, 0, 0, 128), (VALUE, 0, 0, 128),
    (KEY, 1, 0, 128), (QUERY, 1, 0, 128), (VALUE, 1, 0, 128),
)
GOING = ((0, 0, 128), (1, 0, 64), (1, 64, 64))
AHEAD = 3

LEFT_OUT = ((2, 8, 10), ())


def spots(left_out):
    return tuple(offset for offset in range(1, SEQ) if offset not in left_out)


def serves(plan, left_out):
    offset = (plan // BPG - jnp.arange(plan.shape[0], dtype=jnp.int32) // BPG) % SEQ
    moved = (offset[None, :] - jnp.arange(SEQ, dtype=jnp.int32)[:, None]) % SEQ
    misses = functools.reduce(jnp.logical_or, [moved == one for one in left_out])
    return jnp.min(jnp.sum(misses.astype(jnp.int32), axis=1)) == 0


def fill_tables(left_out, plan, here, columns):
    cells = CAP * (SEQ - len(left_out))
    wide = (1, SEQ * BPG)
    lane = lax.broadcasted_iota(jnp.int32, wide, 1)
    source, ids = lane // BPG, lane % BPG
    dest, slot = plan[...] // BPG, plan[...] % BPG
    straight = (dest - source) % SEQ
    shift = jnp.zeros((1, 1), jnp.int32)
    if left_out:
        tried = lax.broadcasted_iota(jnp.int32, (SEQ, SEQ * BPG), 0)
        moved = (straight - tried) % SEQ
        misses = functools.reduce(jnp.add, [(moved == one).astype(jnp.int32) for one in left_out])
        misses = jnp.sum(misses, axis=1, keepdims=True)
        rows = lax.broadcasted_iota(jnp.int32, (SEQ, 1), 0)
        shift = jnp.min(jnp.where(misses == 0, rows, SEQ - 1), axis=0, keepdims=True)
    rank = jnp.zeros(wide, jnp.int32)
    for back in range(1, BPG):
        earlier = pltpu.roll(dest, back, 1)
        rank = rank + ((earlier == dest) & (ids >= back)).astype(jnp.int32)
    place = (dest - shift) % SEQ
    offset = (straight - shift) % SEQ
    spot = offset
    for one in left_out:
        spot = spot - (offset > one).astype(jnp.int32)
    cell = spot * CAP + rank
    going, coming = source == here, place == here

    def pick(count, chosen, key, value, limit):
        rows = lax.broadcasted_iota(jnp.int32, (count, SEQ * BPG), 0)
        picked = jnp.sum(jnp.where(chosen & (key == rows), value, 0), axis=1, keepdims=True)
        return jnp.minimum(picked, limit - 1)

    found = jnp.concatenate(
        [
            jnp.pad(pick(cells, going, cell, ids, BPG), ((0, SEQ * CAP - cells), (0, 0))),
            pick(BPG, coming, slot, cell, cells),
            jnp.pad(pick(cells, coming, cell, slot, BPG), ((0, SEQ * CAP - cells), (0, 0))),
            pick(BPG, going, ids, cell, cells),
            jnp.broadcast_to(shift, (BLOCK - SHIFT, 1)),
        ],
        axis=0,
    )
    columns[...] = jnp.broadcast_to(found, (BLOCK, BLOCK)).T[:8]


PACK, PLACE, REPACK, RETURN, SHIFT = 0, 32, 48, 80, 96


def kernel(left_out, plan, lengths, q_in, k_in, v_in, out, *scratch):
    scratch = list(scratch)

    def take(count):
        taken, scratch[:] = scratch[:count], scratch[count:]
        return taken

    zbuf, xbuf, pbuf = (take(len(COMING)) for _ in range(3))
    opack, rbuf, zpack = (take(len(GOING)) for _ in range(3))
    obuf = take(HEADS_HERE)
    qg, kg, vg, columns, table, t_sem, z_send, z_recv, x_send, x_recv, y_send, y_recv, w_send, w_recv = scratch
    inputs = (q_in, k_in, v_in)
    offsets = spots(left_out)
    s = lax.axis_index("seq")
    h = lax.axis_index("head")

    def across(offset):
        return (lax.rem(s + offset, SEQ), h)

    def peer(step):
        return lax.rem(h + step, HEAD)

    barrier = pltpu.get_barrier_semaphore()
    partners = sorted({offset for one in offsets for offset in (one, SEQ - one)})
    for step in range(1, HEAD):
        pl.semaphore_signal(barrier, inc=1, device_id=(s, peer(step)), device_id_type=MESH)
    for offset in partners:
        pl.semaphore_signal(barrier, inc=1, device_id=across(offset), device_id_type=MESH)
    fill_tables(left_out, plan, s, columns)
    fetch = pltpu.make_async_copy(columns, table, t_sem)
    fetch.start()
    kg[: PAD * BLOCK] = jnp.zeros((PAD * BLOCK, HEAD_DIM), jnp.bfloat16)
    vg[: PAD * BLOCK, :HEAD_DIM] = jnp.zeros((PAD * BLOCK, HEAD_DIM), jnp.bfloat16)
    vg[:, HEAD_DIM:] = jnp.ones(((PAD + BPG) * BLOCK, HEAD_DIM), jnp.bfloat16)
    pl.semaphore_wait(barrier, len(partners) + HEAD - 1)

    def columns_of(device, head):
        return pl.ds(pl.multiple_of((device * HEADS_HERE + head) * HEAD_DIM, HEAD_DIM), HEAD_DIM)

    def wait_for(ref, sem):
        pltpu.make_async_copy(ref, ref, sem).wait()

    def z_start(u):
        tensor, head, row, rows = COMING[u]
        for step in range(1, HEAD):
            to = peer(step)
            pltpu.make_async_remote_copy(
                src_ref=inputs[tensor].at[:, pl.ds(row, rows), columns_of(to, head)],
                dst_ref=zbuf[u].at[pl.ds(h * CAP, CAP)],
                send_sem=z_send.at[u],
                recv_sem=z_recv.at[u],
                device_id=(s, to),
                device_id_type=MESH,
            ).start()
        pltpu.make_async_copy(
            inputs[tensor].at[:, pl.ds(row, rows), columns_of(h, head)], zbuf[u].at[pl.ds(h * CAP, CAP)], z_recv.at[u]
        ).start()

    def z_wait(u):
        wait_for(zbuf[u], z_recv.at[u])

    def x_start(u):
        for spot, offset in enumerate(offsets):
            for j in range(CAP):
                pbuf[u][spot * CAP + j] = zbuf[u][table[0, PACK + (spot + 1) * CAP + j]]
            pltpu.make_async_remote_copy(
                src_ref=pbuf[u].at[pl.ds(spot * CAP, CAP)],
                dst_ref=xbuf[u].at[pl.ds((spot + 1) * CAP, CAP)],
                send_sem=x_send.at[u],
                recv_sem=x_recv.at[u],
                device_id=across(offset),
                device_id_type=MESH,
            ).start()
        for j in range(CAP):
            xbuf[u][j] = zbuf[u][table[0, PACK + j]]

    def x_wait(u):
        wait_for(xbuf[u].at[pl.ds(CAP, len(offsets) * CAP)], x_recv.at[u])

    def attend(head):
        group = lax.rem(s + table[0, SHIFT], SEQ)
        first_end = lengths[0, group]
        second_end = first_end + lengths[1, group]

        def gather(r, carry):
            index = table[0, PLACE + r]
            for u, (tensor, own, row, rows) in enumerate(COMING):
                if own != head:
                    continue
                ahead = 0 if tensor == QUERY else PAD * BLOCK
                at = pl.ds(pl.multiple_of(r * BLOCK + (ahead + row), rows), rows)
                if tensor == VALUE:
                    vg[at, :HEAD_DIM] = xbuf[u][index]
                else:
                    (qg, kg)[tensor][at] = xbuf[u][index]
            return carry

        lax.fori_loop(0, BPG, gather, 0)
        behind = lax.broadcasted_iota(jnp.int32, (1, WINDOW), 1) // BLOCK - PAD
        down = lax.broadcasted_iota(jnp.int32, (BLOCK, BLOCK), 0)
        along = lax.broadcasted_iota(jnp.int32, (BLOCK, BLOCK), 1)
        corner = jnp.where(along <= down, 0.0, -1e30).astype(jnp.float32)

        def record(index):
            return (index >= first_end).astype(jnp.int32) + (index >= second_end).astype(jnp.int32)

        def block(i, carry):
            theirs = behind + i
            seen = (record(theirs) == record(jnp.full_like(theirs, i))) & (theirs >= 0)
            bias = jnp.where(seen, 0.0, -1e30).astype(jnp.float32)
            rows = pl.ds(pl.multiple_of(i * BLOCK, BLOCK), BLOCK)
            window = pl.ds(pl.multiple_of(i * BLOCK, BLOCK), WINDOW)
            scores = lax.dot_general(
                qg[rows], kg[window], (((1,), (1,)), ((), ())), preferred_element_type=jnp.float32
            )
            scores = jnp.concatenate(
                [scores[:, : WINDOW - BLOCK] + bias[:, : WINDOW - BLOCK], scores[:, WINDOW - BLOCK :] + corner], axis=1
            )
            peak = jnp.max(scores, axis=1, keepdims=True)
            weights = jnp.exp2((scores - peak) * (SCALE * LOG2E)).astype(jnp.bfloat16)
            both = jnp.dot(weights, vg[window], preferred_element_type=jnp.float32)
            obuf[head][i] = (both[:, :HEAD_DIM] / both[:, HEAD_DIM:]).astype(jnp.bfloat16)
            return carry

        lax.fori_loop(0, BPG, block, 0, unroll=4)

    def y_start(w):
        head, row, rows = GOING[w]
        for spot, offset in enumerate(offsets):
            for j in range(CAP):
                opack[w][spot * CAP + j] = obuf[head][table[0, REPACK + (spot + 1) * CAP + j], row : row + rows]
            pltpu.make_async_remote_copy(
                src_ref=opack[w].at[pl.ds(spot * CAP, CAP)],
                dst_ref=rbuf[w].at[pl.ds((spot + 1) * CAP, CAP)],
                send_sem=y_send.at[w],
                recv_sem=y_recv.at[w],
                device_id=across(SEQ - offset),
                device_id_type=MESH,
            ).start()
        for j in range(CAP):
            rbuf[w][j] = obuf[head][table[0, REPACK + j], row : row + rows]

    def w_start(w):
        head, row, rows = GOING[w]
        wait_for(rbuf[w].at[pl.ds(CAP, len(offsets) * CAP)], y_recv.at[w])
        for step in range(1, HEAD + 1):
            to = peer(step)
            for j in range(CAP):
                zpack[w][to, j] = rbuf[w][table[0, RETURN + to * CAP + j]]
            target = out.at[:, pl.ds(row, rows), columns_of(h, head)]
            if step == HEAD:
                pltpu.make_async_copy(zpack[w].at[to], target, w_recv.at[w]).start()
                continue
            pltpu.make_async_remote_copy(
                src_ref=zpack[w].at[to],
                dst_ref=target,
                send_sem=w_send.at[w],
                recv_sem=w_recv.at[w],
                device_id=(s, to),
                device_id_type=MESH,
            ).start()

    for u in range(AHEAD):
        z_start(u)
    fetch.wait()
    for u in range(len(COMING)):
        z_wait(u)
        x_start(u)
        if u + AHEAD < len(COMING):
            z_start(u + AHEAD)
    first = [u for u, unit in enumerate(COMING) if unit[1] == 0]
    second = [u for u, unit in enumerate(COMING) if unit[1] == 1]
    for u in first:
        x_wait(u)
    attend(0)
    for u in second[:-1]:
        x_wait(u)
    y_start(0)
    x_wait(second[-1])
    attend(1)
    for w in range(1, len(GOING)):
        y_start(w)
    for w in range(len(GOING)):
        w_start(w)
    for u in range(len(COMING)):
        wait_for(zbuf[u].at[pl.ds(0, (HEAD - 1) * CAP)], z_send.at[u])
        wait_for(pbuf[u], x_send.at[u])
    for w, (_, row, rows) in enumerate(GOING):
        wait_for(opack[w], y_send.at[w])
        wait_for(zpack[w].at[pl.ds(0, HEAD - 1)], w_send.at[w])
        wait_for(out.at[:, pl.ds(row, rows), pl.ds(0, HEAD * HEAD_DIM)], w_recv.at[w])


def exchange(number, left_out, queries, keys, values, lengths, plan):
    bf16 = jnp.bfloat16
    count = len(spots(left_out))

    def blocks(many, rows):
        return pltpu.VMEM((many, rows, HEAD_DIM), bf16)

    def in_flight(units):
        return pltpu.SemaphoreType.DMA((len(units),))

    return pl.pallas_call(
        functools.partial(kernel, left_out),
        out_shape=jax.ShapeDtypeStruct(queries.shape, bf16),
        in_specs=[pl.BlockSpec(memory_space=pltpu.VMEM), pl.BlockSpec(memory_space=pltpu.SMEM)]
        + [pl.BlockSpec(memory_space=pl.ANY)] * 3,
        out_specs=pl.BlockSpec(memory_space=pl.ANY),
        scratch_shapes=[blocks(BPG, unit[3]) for unit in COMING]
        + [blocks((count + 1) * CAP, unit[3]) for unit in COMING]
        + [blocks(count * CAP, unit[3]) for unit in COMING]
        + [blocks(count * CAP, unit[2]) for unit in GOING]
        + [blocks((count + 1) * CAP, unit[2]) for unit in GOING]
        + [pltpu.VMEM((HEAD, CAP, unit[2], HEAD_DIM), bf16) for unit in GOING]
        + [blocks(BPG, BLOCK)] * HEADS_HERE
        + [
            pltpu.VMEM((BPG * BLOCK, HEAD_DIM), bf16),
            pltpu.VMEM(((PAD + BPG) * BLOCK, HEAD_DIM), bf16),
            pltpu.VMEM(((PAD + BPG) * BLOCK, 2 * HEAD_DIM), bf16),
            pltpu.VMEM((8, BLOCK), jnp.int32),
            pltpu.SMEM((8, BLOCK), jnp.int32),
            pltpu.SemaphoreType.DMA,
        ]
        + [in_flight(COMING)] * 4
        + [in_flight(GOING)] * 4,
        compiler_params=pltpu.CompilerParams(
            collective_id=number, has_side_effects=True, vmem_limit_bytes=63 * 2**20
        ),
        cost_estimate=pl.CostEstimate(flops=2_000_000_000, bytes_accessed=4 * 2**20, transcendentals=4_000_000),
    )(plan.reshape(1, -1), lengths.T, queries, keys, values)


def local(queries, keys, values, lengths, plan):
    queries, keys, values = (array.reshape(CAP, BLOCK, -1) for array in (queries, keys, values))
    forms = [functools.partial(exchange, number, left_out) for number, left_out in enumerate(LEFT_OUT)]
    attended = lax.cond(serves(plan, LEFT_OUT[0]), *forms, queries, keys, values, lengths, plan)
    return attended.reshape(CAP * BLOCK, -1)


def solution(mesh):
    placed = (
        P(("seq", "head"), None),
        P(("seq", "head"), None),
        P(("seq", "head"), None),
        P(),
        P(),
    )
    return jax.shard_map(
        local, mesh=mesh, in_specs=placed, out_specs=P(("seq", "head"), None), check_vma=False
    )
```

```python
import functools
import math

import jax
import jax.numpy as jnp
from jax import lax
from jax.experimental import pallas as pl
from jax.experimental.pallas import tpu as pltpu
from jax.sharding import PartitionSpec as P

HEAD_DIM = 128
BLOCK = 128
SEQ = 16
HEAD = 8
BPG = 16
CAP = 2
LONGEST = 10
HEADS_HERE = 2
PAD = LONGEST - 1
WINDOW = LONGEST * BLOCK
MESH = pl.DeviceIdType.MESH
SCALE = 1.0 / math.sqrt(HEAD_DIM)
LOG2E = 1.4426950408889634
QUERY, KEY, VALUE = 0, 1, 2

COMING = (
    (KEY, 0, 0, 64), (KEY, 0, 64, 64), (QUERY, 0, 0, 128), (VALUE, 0, 0, 128),
    (KEY, 1, 0, 128), (QUERY, 1, 0, 128), (VALUE, 1, 0, 128),
)
GOING = ((0, 0, 128), (1, 0, 64), (1, 64, 64))
AHEAD = 3

FORMS = (
    (2, 6, 8, 9, 10), (6, 7, 8, 13, 14), (2, 7, 8, 10, 14), (5, 6, 8, 10, 14),
    (3, 6, 8, 9, 14), (3, 6, 8, 10, 13), (2, 6, 8, 10, 11), (6, 8, 14), (),
)


def spots(left_out):
    return tuple(offset for offset in range(1, SEQ) if offset not in left_out)


def first_form(plan):
    offset = (plan // BPG - jnp.arange(plan.shape[0], dtype=jnp.int32) // BPG) % SEQ
    shift = jnp.arange(SEQ, dtype=jnp.int32)
    moved = (offset[None, :] - shift[:, None]) % SEQ
    against = jnp.zeros_like(moved)
    for one in range(1, SEQ):
        against = jnp.where(moved == one, sum(1 << n for n, left_out in enumerate(FORMS) if one in left_out), against)
    against = lax.reduce(against, jnp.int32(0), lax.bitwise_or, (1,))
    form = jnp.full((SEQ,), len(FORMS) - 1, jnp.int32)
    for number in reversed(range(len(FORMS) - 1)):
        form = jnp.where(against & (1 << number) == 0, number, form)
    return jnp.min(form)


def fill_tables(left_out, plan, here, columns):
    cells = CAP * (SEQ - len(left_out))
    wide = (1, SEQ * BPG)
    lane = lax.broadcasted_iota(jnp.int32, wide, 1)
    source, ids = lane // BPG, lane % BPG
    dest, slot = plan[...] // BPG, plan[...] % BPG
    straight = (dest - source) % SEQ
    shift = jnp.zeros((1, 1), jnp.int32)
    if left_out:
        tried = lax.broadcasted_iota(jnp.int32, (SEQ, SEQ * BPG), 0)
        moved = (straight - tried) % SEQ
        misses = functools.reduce(jnp.add, [(moved == one).astype(jnp.int32) for one in left_out])
        misses = jnp.sum(misses, axis=1, keepdims=True)
        rows = lax.broadcasted_iota(jnp.int32, (SEQ, 1), 0)
        shift = jnp.min(jnp.where(misses == 0, rows, SEQ - 1), axis=0, keepdims=True)
    rank = jnp.zeros(wide, jnp.int32)
    for back in range(1, BPG):
        earlier = pltpu.roll(dest, back, 1)
        rank = rank + ((earlier == dest) & (ids >= back)).astype(jnp.int32)
    place = (dest - shift) % SEQ
    offset = (straight - shift) % SEQ
    spot = offset
    for one in left_out:
        spot = spot - (offset > one).astype(jnp.int32)
    cell = spot * CAP + rank
    going, coming = source == here, place == here

    def pick(count, chosen, key, value, limit):
        rows = lax.broadcasted_iota(jnp.int32, (count, SEQ * BPG), 0)
        picked = jnp.sum(jnp.where(chosen & (key == rows), value, 0), axis=1, keepdims=True)
        return jnp.minimum(picked, limit - 1)

    found = jnp.concatenate(
        [
            jnp.pad(pick(cells, going, cell, ids, BPG), ((0, SEQ * CAP - cells), (0, 0))),
            pick(BPG, coming, slot, cell, cells),
            jnp.pad(pick(cells, coming, cell, slot, BPG), ((0, SEQ * CAP - cells), (0, 0))),
            pick(BPG, going, ids, cell, cells),
            jnp.broadcast_to(shift, (BLOCK - SHIFT, 1)),
        ],
        axis=0,
    )
    columns[...] = jnp.broadcast_to(found, (BLOCK, BLOCK)).T[:8]


PACK, PLACE, REPACK, RETURN, SHIFT = 0, 32, 48, 80, 96


def kernel(left_out, plan, lengths, q_in, k_in, v_in, out, *scratch):
    scratch = list(scratch)

    def take(count):
        taken, scratch[:] = scratch[:count], scratch[count:]
        return taken

    zbuf, xbuf, pbuf = (take(len(COMING)) for _ in range(3))
    opack, rbuf, zpack = (take(len(GOING)) for _ in range(3))
    obuf, qg, kg, vg, columns, table, t_sem, z_send, z_recv, x_send, x_recv, y_send, y_recv, w_send, w_recv = scratch
    inputs = (q_in, k_in, v_in)
    offsets = spots(left_out)
    s = lax.axis_index("seq")
    h = lax.axis_index("head")

    def across(offset):
        return (lax.rem(s + offset, SEQ), h)

    def offset_of(spot):
        offset = spot
        for one in left_out:
            offset = offset + (offset >= one).astype(jnp.int32)
        return offset

    def each(first, last, body):
        def step(i, carry):
            body(i)
            return carry

        lax.fori_loop(first, last, step, 0)

    def peer(step):
        return lax.rem(h + step, HEAD)

    barrier = pltpu.get_barrier_semaphore()
    partners = sorted({offset for one in offsets for offset in (one, SEQ - one)})
    for step in range(1, HEAD):
        pl.semaphore_signal(barrier, inc=1, device_id=(s, peer(step)), device_id_type=MESH)
    for offset in partners:
        pl.semaphore_signal(barrier, inc=1, device_id=across(offset), device_id_type=MESH)
    fill_tables(left_out, plan, s, columns)
    fetch = pltpu.make_async_copy(columns, table, t_sem)
    fetch.start()
    kg[: PAD * BLOCK] = jnp.zeros((PAD * BLOCK, HEAD_DIM), jnp.bfloat16)
    vg[: PAD * BLOCK, :HEAD_DIM] = jnp.zeros((PAD * BLOCK, HEAD_DIM), jnp.bfloat16)
    vg[:, HEAD_DIM:] = jnp.ones(((PAD + BPG) * BLOCK, HEAD_DIM), jnp.bfloat16)
    pl.semaphore_wait(barrier, len(partners) + HEAD - 1)

    def columns_of(device, head):
        return pl.ds(pl.multiple_of((device * HEADS_HERE + head) * HEAD_DIM, HEAD_DIM), HEAD_DIM)

    def wait_for(ref, sem):
        pltpu.make_async_copy(ref, ref, sem).wait()

    def z_start(u):
        tensor, head, row, rows = COMING[u]

        def send(step):
            to = peer(step)
            pltpu.make_async_remote_copy(
                src_ref=inputs[tensor].at[:, pl.ds(row, rows), columns_of(to, head)],
                dst_ref=zbuf[u].at[pl.ds(h * CAP, CAP)],
                send_sem=z_send.at[u],
                recv_sem=z_recv.at[u],
                device_id=(s, to),
                device_id_type=MESH,
            ).start()

        each(1, HEAD, send)
        pltpu.make_async_copy(
            inputs[tensor].at[:, pl.ds(row, rows), columns_of(h, head)], zbuf[u].at[pl.ds(h * CAP, CAP)], z_recv.at[u]
        ).start()

    def z_wait(u):
        wait_for(zbuf[u], z_recv.at[u])

    def x_start(u):
        def send(spot):
            for j in range(CAP):
                pbuf[u][(spot - 1) * CAP + j] = zbuf[u][table[0, PACK + spot * CAP + j]]
            pltpu.make_async_remote_copy(
                src_ref=pbuf[u].at[pl.ds((spot - 1) * CAP, CAP)],
                dst_ref=xbuf[u].at[pl.ds(spot * CAP, CAP)],
                send_sem=x_send.at[u],
                recv_sem=x_recv.at[u],
                device_id=across(offset_of(spot)),
                device_id_type=MESH,
            ).start()

        each(1, len(offsets) + 1, send)
        for j in range(CAP):
            xbuf[u][j] = zbuf[u][table[0, PACK + j]]

    def x_wait(u):
        wait_for(xbuf[u].at[pl.ds(CAP, len(offsets) * CAP)], x_recv.at[u])

    def collect(head):
        def gather(r, carry):
            index = table[0, PLACE + r]
            for u, (tensor, own, row, rows) in enumerate(COMING):
                if own != head:
                    continue
                ahead = 0 if tensor == QUERY else PAD * BLOCK
                at = pl.ds(pl.multiple_of(r * BLOCK + (ahead + row), rows), rows)
                if tensor == VALUE:
                    vg[at, :HEAD_DIM] = xbuf[u][index]
                else:
                    (qg, kg)[tensor][at] = xbuf[u][index]
            return carry

        lax.fori_loop(0, BPG, gather, 0)

    def attend(head):
        group = lax.rem(s + table[0, SHIFT], SEQ)
        first_end = lengths[0, group]
        second_end = first_end + lengths[1, group]
        behind = lax.broadcasted_iota(jnp.int32, (1, WINDOW), 1) // BLOCK - PAD
        down = lax.broadcasted_iota(jnp.int32, (BLOCK, BLOCK), 0)
        along = lax.broadcasted_iota(jnp.int32, (BLOCK, BLOCK), 1)
        corner = jnp.where(along <= down, 0.0, -1e30).astype(jnp.float32)

        def record(index):
            return (index >= first_end).astype(jnp.int32) + (index >= second_end).astype(jnp.int32)

        def block(i, carry):
            theirs = behind + i
            seen = (record(theirs) == record(jnp.full_like(theirs, i))) & (theirs >= 0)
            bias = jnp.where(seen, 0.0, -1e30).astype(jnp.float32)
            rows = pl.ds(pl.multiple_of(i * BLOCK, BLOCK), BLOCK)
            window = pl.ds(pl.multiple_of(i * BLOCK, BLOCK), WINDOW)
            scores = lax.dot_general(
                qg[rows], kg[window], (((1,), (1,)), ((), ())), preferred_element_type=jnp.float32
            )
            scores = jnp.concatenate(
                [scores[:, : WINDOW - BLOCK] + bias[:, : WINDOW - BLOCK], scores[:, WINDOW - BLOCK :] + corner], axis=1
            )
            peak = jnp.max(scores, axis=1, keepdims=True)
            weights = jnp.exp2((scores - peak) * (SCALE * LOG2E)).astype(jnp.bfloat16)
            both = jnp.dot(weights, vg[window], preferred_element_type=jnp.float32)
            obuf[head * BPG + i] = (both[:, :HEAD_DIM] / both[:, HEAD_DIM:]).astype(jnp.bfloat16)
            return carry

        lax.fori_loop(0, BPG, block, 0, unroll=4)

    def y_start(w):
        head, row, rows = GOING[w]

        def send(spot):
            for j in range(CAP):
                opack[w][(spot - 1) * CAP + j] = obuf[table[0, REPACK + spot * CAP + j] + head * BPG, row : row + rows]
            pltpu.make_async_remote_copy(
                src_ref=opack[w].at[pl.ds((spot - 1) * CAP, CAP)],
                dst_ref=rbuf[w].at[pl.ds(spot * CAP, CAP)],
                send_sem=y_send.at[w],
                recv_sem=y_recv.at[w],
                device_id=across(SEQ - offset_of(spot)),
                device_id_type=MESH,
            ).start()

        each(1, len(offsets) + 1, send)
        for j in range(CAP):
            rbuf[w][j] = obuf[table[0, REPACK + j] + head * BPG, row : row + rows]

    def w_start(w):
        head, row, rows = GOING[w]
        wait_for(rbuf[w].at[pl.ds(CAP, len(offsets) * CAP)], y_recv.at[w])
        target = out.at[:, pl.ds(row, rows), columns_of(h, head)]

        def pack(to):
            for j in range(CAP):
                zpack[w][to, j] = rbuf[w][table[0, RETURN + to * CAP + j]]

        def send(step):
            to = peer(step)
            pack(to)
            pltpu.make_async_remote_copy(
                src_ref=zpack[w].at[to],
                dst_ref=target,
                send_sem=w_send.at[w],
                recv_sem=w_recv.at[w],
                device_id=(s, to),
                device_id_type=MESH,
            ).start()

        each(1, HEAD, send)
        pack(h)
        pltpu.make_async_copy(zpack[w].at[h], target, w_recv.at[w]).start()

    for u in range(AHEAD):
        z_start(u)
    fetch.wait()
    for u in range(len(COMING)):
        z_wait(u)
        x_start(u)
        if u + AHEAD < len(COMING):
            z_start(u + AHEAD)
    first = [u for u, unit in enumerate(COMING) if unit[1] == 0]
    second = [u for u, unit in enumerate(COMING) if unit[1] == 1]

    def one_head(head):
        @pl.when(head == 0)
        def _():
            for u in first:
                x_wait(u)
            collect(0)

        @pl.when(head == 1)
        def _():
            for u in second[:-1]:
                x_wait(u)
            y_start(0)
            x_wait(second[-1])
            collect(1)

        attend(head)

    each(0, HEADS_HERE, one_head)
    for w in range(1, len(GOING)):
        y_start(w)
    for w in range(len(GOING)):
        w_start(w)
    for u in range(len(COMING)):
        wait_for(zbuf[u].at[pl.ds(0, (HEAD - 1) * CAP)], z_send.at[u])
        wait_for(pbuf[u], x_send.at[u])
    for w, (_, row, rows) in enumerate(GOING):
        wait_for(opack[w], y_send.at[w])
        wait_for(zpack[w].at[pl.ds(0, HEAD - 1)], w_send.at[w])
        wait_for(out.at[:, pl.ds(row, rows), pl.ds(0, HEAD * HEAD_DIM)], w_recv.at[w])


def exchange(number, left_out, queries, keys, values, lengths, plan):
    bf16 = jnp.bfloat16
    count = len(spots(left_out))

    def blocks(many, rows):
        return pltpu.VMEM((many, rows, HEAD_DIM), bf16)

    def in_flight(units):
        return pltpu.SemaphoreType.DMA((len(units),))

    return pl.pallas_call(
        functools.partial(kernel, left_out),
        out_shape=jax.ShapeDtypeStruct(queries.shape, bf16),
        in_specs=[pl.BlockSpec(memory_space=pltpu.VMEM), pl.BlockSpec(memory_space=pltpu.SMEM)]
        + [pl.BlockSpec(memory_space=pl.ANY)] * 3,
        out_specs=pl.BlockSpec(memory_space=pl.ANY),
        scratch_shapes=[blocks(BPG, unit[3]) for unit in COMING]
        + [blocks((count + 1) * CAP, unit[3]) for unit in COMING]
        + [blocks(count * CAP, unit[3]) for unit in COMING]
        + [blocks(count * CAP, unit[2]) for unit in GOING]
        + [blocks((count + 1) * CAP, unit[2]) for unit in GOING]
        + [pltpu.VMEM((HEAD, CAP, unit[2], HEAD_DIM), bf16) for unit in GOING]
        + [
            blocks(HEADS_HERE * BPG, BLOCK),
            pltpu.VMEM((BPG * BLOCK, HEAD_DIM), bf16),
            pltpu.VMEM(((PAD + BPG) * BLOCK, HEAD_DIM), bf16),
            pltpu.VMEM(((PAD + BPG) * BLOCK, 2 * HEAD_DIM), bf16),
            pltpu.VMEM((8, BLOCK), jnp.int32),
            pltpu.SMEM((8, BLOCK), jnp.int32),
            pltpu.SemaphoreType.DMA,
        ]
        + [in_flight(COMING)] * 4
        + [in_flight(GOING)] * 4,
        compiler_params=pltpu.CompilerParams(
            collective_id=number, has_side_effects=True, vmem_limit_bytes=50 * 2**20
        ),
        cost_estimate=pl.CostEstimate(flops=2_000_000_000, bytes_accessed=4 * 2**20, transcendentals=4_000_000),
    )(plan.reshape(1, -1), lengths.T, queries, keys, values)


def local(queries, keys, values, lengths, plan):
    queries, keys, values = (array.reshape(CAP, BLOCK, -1) for array in (queries, keys, values))
    forms = [functools.partial(exchange, number, left_out) for number, left_out in enumerate(FORMS)]
    attended = lax.switch(first_form(plan), forms, queries, keys, values, lengths, plan)
    return attended.reshape(CAP * BLOCK, -1)


def solution(mesh):
    placed = (
        P(("seq", "head"), None),
        P(("seq", "head"), None),
        P(("seq", "head"), None),
        P(),
        P(),
    )
    return jax.shard_map(
        local, mesh=mesh, in_specs=placed, out_specs=P(("seq", "head"), None), check_vma=False
    )
```

```python
import functools
import math

import jax
import jax.numpy as jnp
from jax import lax
from jax.experimental import pallas as pl
from jax.experimental.pallas import tpu as pltpu
from jax.sharding import PartitionSpec as P

HEAD_DIM = 128
BLOCK = 128
SEQ = 16
SIDE = 4
HEAD = 8
BPG = 16
CAP = 2
LONGEST = 10
HEADS_HERE = 2
PAD = LONGEST - 1
WINDOW = LONGEST * BLOCK
MESH = pl.DeviceIdType.MESH
SCALE = 1.0 / math.sqrt(HEAD_DIM)
LOG2E = 1.4426950408889634
QUERY, KEY, VALUE = 0, 1, 2

COMING = (
    (KEY, 0, 0, 64),
    (KEY, 0, 64, 64),
    (QUERY, 0, 0, 64),
    (QUERY, 0, 64, 64),
    (VALUE, 0, 0, 64),
    (VALUE, 0, 64, 64),
    (KEY, 1, 0, 128),
    (QUERY, 1, 0, 128),
    (VALUE, 1, 0, 64),
    (VALUE, 1, 64, 64),
)
GOING = ((0, 0, 128), (1, 0, 64), (1, 64, 64))
AHEAD = 5

FORMS = (
    (2, 6, 8, 9, 10), (6, 7, 8, 13, 14), (2, 7, 8, 10, 14), (5, 6, 8, 10, 14),
    (3, 6, 8, 9, 14), (3, 6, 8, 10, 13), (2, 6, 8, 10, 11), (6, 8, 14), (),
)


def spots(left_out):
    return tuple(offset for offset in range(1, SEQ) if offset not in left_out)


def first_form(plan):
    offset = (plan // BPG - jnp.arange(plan.shape[0], dtype=jnp.int32) // BPG) % SEQ
    shift = jnp.arange(SEQ, dtype=jnp.int32)
    moved = (offset[None, :] - shift[:, None]) % SEQ
    against = jnp.zeros_like(moved)
    for one in range(1, SEQ):
        against = jnp.where(moved == one, sum(1 << n for n, left_out in enumerate(FORMS) if one in left_out), against)
    against = lax.reduce(against, jnp.int32(0), lax.bitwise_or, (1,))
    form = jnp.full((SEQ,), len(FORMS) - 1, jnp.int32)
    for number in reversed(range(len(FORMS) - 1)):
        form = jnp.where(against & (1 << number) == 0, number, form)
    return jnp.min(form)


def fill_tables(left_out, plan, here, columns):
    cells = CAP * (SEQ - len(left_out))
    wide = (1, SEQ * BPG)
    lane = lax.broadcasted_iota(jnp.int32, wide, 1)
    source, ids = lane // BPG, lane % BPG
    dest, slot = plan[...] // BPG, plan[...] % BPG
    straight = (dest - source) % SEQ
    shift = jnp.zeros((1, 1), jnp.int32)
    if left_out:
        tried = lax.broadcasted_iota(jnp.int32, (SEQ, SEQ * BPG), 0)
        moved = (straight - tried) % SEQ
        misses = functools.reduce(jnp.add, [(moved == one).astype(jnp.int32) for one in left_out])
        misses = jnp.sum(misses, axis=1, keepdims=True)
        rows = lax.broadcasted_iota(jnp.int32, (SEQ, 1), 0)
        shift = jnp.min(jnp.where(misses == 0, rows, SEQ - 1), axis=0, keepdims=True)
    rank = jnp.zeros(wide, jnp.int32)
    for back in range(1, BPG):
        earlier = pltpu.roll(dest, back, 1)
        rank = rank + ((earlier == dest) & (ids >= back)).astype(jnp.int32)
    place = (dest - shift) % SEQ
    offset = (straight - shift) % SEQ
    spot = offset
    for one in left_out:
        spot = spot - (offset > one).astype(jnp.int32)
    cell = spot * CAP + rank
    going, coming = source == here, place == here

    def pick(count, chosen, key, value, limit):
        rows = lax.broadcasted_iota(jnp.int32, (count, SEQ * BPG), 0)
        picked = jnp.sum(jnp.where(chosen & (key == rows), value, 0), axis=1, keepdims=True)
        return jnp.minimum(picked, limit - 1)

    found = jnp.concatenate(
        [
            jnp.pad(pick(cells, going, cell, ids, BPG), ((0, SEQ * CAP - cells), (0, 0))),
            pick(BPG, coming, slot, cell, cells),
            jnp.pad(pick(cells, coming, cell, slot, BPG), ((0, SEQ * CAP - cells), (0, 0))),
            pick(BPG, going, ids, cell, cells),
            jnp.broadcast_to(shift, (BLOCK - SHIFT, 1)),
        ],
        axis=0,
    )
    columns[...] = jnp.broadcast_to(found, (BLOCK, BLOCK)).T[:8]


PACK, PLACE, REPACK, RETURN, SHIFT = 0, 32, 48, 80, 96


def kernel(left_out, plan, lengths, q_in, k_in, v_in, out, *scratch):
    scratch = list(scratch)

    def take(count):
        taken, scratch[:] = scratch[:count], scratch[count:]
        return taken

    zbuf, xbuf, pbuf = (take(len(COMING)) for _ in range(3))
    opack, rbuf, zpack = (take(len(GOING)) for _ in range(3))
    obuf, qg, kg, vg, columns, table, t_sem, all_in, z_send, z_recv, x_send, x_recv, y_send, y_recv, w_send, w_recv = scratch
    inputs = (q_in, k_in, v_in)
    offsets = spots(left_out)
    s = lax.axis_index("seq")
    h = lax.axis_index("head")

    def across(offset):
        return (lax.rem(s + offset, SEQ), h)

    def offset_of(spot):
        offset = spot
        for one in left_out:
            offset = offset + (offset >= one).astype(jnp.int32)
        return offset

    def each(first, last, body):
        def step(i, carry):
            body(i)
            return carry

        lax.fori_loop(first, last, step, 0)

    def peer(step):
        return lax.rem(h + step, HEAD)

    barrier = pltpu.get_barrier_semaphore()
    for step in range(1, HEAD):
        pl.semaphore_signal(barrier, inc=1, device_id=(s, peer(step)), device_id_type=MESH)
    row, line = s // SIDE, s % SIDE
    beside = [(row * SIDE + lax.rem(line + step, SIDE), h) for step in range(1, SIDE)]
    above = [(lax.rem(row + step, SIDE) * SIDE + line, h) for step in range(1, SIDE)]
    for device in above + beside:
        pl.semaphore_signal(barrier, inc=1, device_id=device, device_id_type=MESH)
    pl.semaphore_wait(barrier, HEAD - 1 + 2 * (SIDE - 1))
    for device in beside:
        pl.semaphore_signal(all_in, inc=1, device_id=device, device_id_type=MESH)

    def columns_of(device, head):
        return pl.ds(pl.multiple_of((device * HEADS_HERE + head) * HEAD_DIM, HEAD_DIM), HEAD_DIM)

    def wait_for(ref, sem):
        pltpu.make_async_copy(ref, ref, sem).wait()

    def z_start(u):
        tensor, head, row, rows = COMING[u]

        def send(step):
            to = peer(step)
            pltpu.make_async_remote_copy(
                src_ref=inputs[tensor].at[:, pl.ds(row, rows), columns_of(to, head)],
                dst_ref=zbuf[u].at[pl.ds(h * CAP, CAP)],
                send_sem=z_send.at[u],
                recv_sem=z_recv.at[u],
                device_id=(s, to),
                device_id_type=MESH,
            ).start()

        each(1, HEAD, send)
        pltpu.make_async_copy(
            inputs[tensor].at[:, pl.ds(row, rows), columns_of(h, head)], zbuf[u].at[pl.ds(h * CAP, CAP)], z_recv.at[u]
        ).start()

    def z_wait(u):
        wait_for(zbuf[u], z_recv.at[u])

    def x_start(u):
        def send(spot):
            for j in range(CAP):
                pbuf[u][(spot - 1) * CAP + j] = zbuf[u][table[0, PACK + spot * CAP + j]]
            pltpu.make_async_remote_copy(
                src_ref=pbuf[u].at[pl.ds((spot - 1) * CAP, CAP)],
                dst_ref=xbuf[u].at[pl.ds(spot * CAP, CAP)],
                send_sem=x_send.at[u],
                recv_sem=x_recv.at[u],
                device_id=across(offset_of(spot)),
                device_id_type=MESH,
            ).start()

        each(1, len(offsets) + 1, send)
        for j in range(CAP):
            xbuf[u][j] = zbuf[u][table[0, PACK + j]]

    def x_wait(u):
        wait_for(xbuf[u].at[pl.ds(CAP, len(offsets) * CAP)], x_recv.at[u])

    def collect(head):
        def gather(r, carry):
            index = table[0, PLACE + r]
            for u, (tensor, own, row, rows) in enumerate(COMING):
                if own != head:
                    continue
                ahead = 0 if tensor == QUERY else PAD * BLOCK
                at = pl.ds(pl.multiple_of(r * BLOCK + (ahead + row), rows), rows)
                if tensor == VALUE:
                    vg[at, :HEAD_DIM] = xbuf[u][index]
                else:
                    (qg, kg)[tensor][at] = xbuf[u][index]
            return carry

        lax.fori_loop(0, BPG, gather, 0)

    def attend(head):
        group = lax.rem(s + table[0, SHIFT], SEQ)
        first_end = lengths[0, group]
        second_end = first_end + lengths[1, group]
        behind = lax.broadcasted_iota(jnp.int32, (1, WINDOW), 1) // BLOCK - PAD
        down = lax.broadcasted_iota(jnp.int32, (BLOCK, BLOCK), 0)
        along = lax.broadcasted_iota(jnp.int32, (BLOCK, BLOCK), 1)
        corner = jnp.where(along <= down, 0.0, -1e30).astype(jnp.float32)

        def record(index):
            return (index >= first_end).astype(jnp.int32) + (index >= second_end).astype(jnp.int32)

        def block(i, carry):
            theirs = behind + i
            seen = (record(theirs) == record(jnp.full_like(theirs, i))) & (theirs >= 0)
            bias = jnp.where(seen, 0.0, -1e30).astype(jnp.float32)
            rows = pl.ds(pl.multiple_of(i * BLOCK, BLOCK), BLOCK)
            window = pl.ds(pl.multiple_of(i * BLOCK, BLOCK), WINDOW)
            scores = lax.dot_general(
                qg[rows], kg[window], (((1,), (1,)), ((), ())), preferred_element_type=jnp.float32
            )
            scores = jnp.concatenate(
                [scores[:, : WINDOW - BLOCK] + bias[:, : WINDOW - BLOCK], scores[:, WINDOW - BLOCK :] + corner], axis=1
            )
            peak = jnp.max(scores, axis=1, keepdims=True)
            weights = jnp.exp2((scores - peak) * (SCALE * LOG2E)).astype(jnp.bfloat16)
            both = jnp.dot(weights, vg[window], preferred_element_type=jnp.float32)
            obuf[head * BPG + i] = (both[:, :HEAD_DIM] / both[:, HEAD_DIM:]).astype(jnp.bfloat16)
            return carry

        lax.fori_loop(0, BPG, block, 0, unroll=8)

    def y_start(w):
        head, row, rows = GOING[w]

        def send(spot):
            for j in range(CAP):
                opack[w][(spot - 1) * CAP + j] = obuf[table[0, REPACK + spot * CAP + j] + head * BPG, row : row + rows]
            pltpu.make_async_remote_copy(
                src_ref=opack[w].at[pl.ds((spot - 1) * CAP, CAP)],
                dst_ref=rbuf[w].at[pl.ds(spot * CAP, CAP)],
                send_sem=y_send.at[w],
                recv_sem=y_recv.at[w],
                device_id=across(SEQ - offset_of(spot)),
                device_id_type=MESH,
            ).start()

        each(1, len(offsets) + 1, send)
        for j in range(CAP):
            rbuf[w][j] = obuf[table[0, REPACK + j] + head * BPG, row : row + rows]

    def w_start(w):
        head, row, rows = GOING[w]
        wait_for(rbuf[w].at[pl.ds(CAP, len(offsets) * CAP)], y_recv.at[w])
        target = out.at[:, pl.ds(row, rows), columns_of(h, head)]

        def pack(to):
            for j in range(CAP):
                zpack[w][to, j] = rbuf[w][table[0, RETURN + to * CAP + j]]

        def send(step):
            to = peer(step)
            pack(to)
            pltpu.make_async_remote_copy(
                src_ref=zpack[w].at[to],
                dst_ref=target,
                send_sem=w_send.at[w],
                recv_sem=w_recv.at[w],
                device_id=(s, to),
                device_id_type=MESH,
            ).start()

        each(1, HEAD, send)
        pack(h)
        pltpu.make_async_copy(zpack[w].at[h], target, w_recv.at[w]).start()

    for u in range(AHEAD):
        z_start(u)
    fill_tables(left_out, plan, s, columns)
    fetch = pltpu.make_async_copy(columns, table, t_sem)
    fetch.start()
    kg[: PAD * BLOCK] = jnp.zeros((PAD * BLOCK, HEAD_DIM), jnp.bfloat16)
    vg[: PAD * BLOCK, :HEAD_DIM] = jnp.zeros((PAD * BLOCK, HEAD_DIM), jnp.bfloat16)
    vg[:, HEAD_DIM:] = jnp.ones(((PAD + BPG) * BLOCK, HEAD_DIM), jnp.bfloat16)
    fetch.wait()
    pl.semaphore_wait(all_in, SIDE - 1)
    for u in range(len(COMING)):
        z_wait(u)
        x_start(u)
        if u + AHEAD < len(COMING):
            z_start(u + AHEAD)
    first = [u for u, unit in enumerate(COMING) if unit[1] == 0]
    second = [u for u, unit in enumerate(COMING) if unit[1] == 1]

    def one_head(head):
        @pl.when(head == 0)
        def _():
            for u in first:
                x_wait(u)
            collect(0)

        @pl.when(head == 1)
        def _():
            for u in second[:-1]:
                x_wait(u)
            y_start(0)
            x_wait(second[-1])
            collect(1)

        attend(head)

    each(0, HEADS_HERE, one_head)
    for w in range(1, len(GOING)):
        y_start(w)
    for w in range(len(GOING)):
        w_start(w)
    for u in range(len(COMING)):
        wait_for(zbuf[u].at[pl.ds(0, (HEAD - 1) * CAP)], z_send.at[u])
        wait_for(pbuf[u], x_send.at[u])
    for w, (_, row, rows) in enumerate(GOING):
        wait_for(opack[w], y_send.at[w])
        wait_for(zpack[w].at[pl.ds(0, HEAD - 1)], w_send.at[w])
        wait_for(out.at[:, pl.ds(row, rows), pl.ds(0, HEAD * HEAD_DIM)], w_recv.at[w])


def exchange(number, left_out, queries, keys, values, lengths, plan):
    bf16 = jnp.bfloat16
    count = len(spots(left_out))

    def blocks(many, rows):
        return pltpu.VMEM((many, rows, HEAD_DIM), bf16)

    def in_flight(units):
        return pltpu.SemaphoreType.DMA((len(units),))

    return pl.pallas_call(
        functools.partial(kernel, left_out),
        out_shape=jax.ShapeDtypeStruct(queries.shape, bf16),
        in_specs=[pl.BlockSpec(memory_space=pltpu.VMEM), pl.BlockSpec(memory_space=pltpu.SMEM)]
        + [pl.BlockSpec(memory_space=pl.ANY)] * 3,
        out_specs=pl.BlockSpec(memory_space=pl.ANY),
        scratch_shapes=[blocks(BPG, unit[3]) for unit in COMING]
        + [blocks((count + 1) * CAP, unit[3]) for unit in COMING]
        + [blocks(count * CAP, unit[3]) for unit in COMING]
        + [blocks(count * CAP, unit[2]) for unit in GOING]
        + [blocks((count + 1) * CAP, unit[2]) for unit in GOING]
        + [pltpu.VMEM((HEAD, CAP, unit[2], HEAD_DIM), bf16) for unit in GOING]
        + [
            blocks(HEADS_HERE * BPG, BLOCK),
            pltpu.VMEM((BPG * BLOCK, HEAD_DIM), bf16),
            pltpu.VMEM(((PAD + BPG) * BLOCK, HEAD_DIM), bf16),
            pltpu.VMEM(((PAD + BPG) * BLOCK, 2 * HEAD_DIM), bf16),
            pltpu.VMEM((8, BLOCK), jnp.int32),
            pltpu.SMEM((8, BLOCK), jnp.int32),
            pltpu.SemaphoreType.DMA,
            pltpu.SemaphoreType.REGULAR,
        ]
        + [in_flight(COMING)] * 4
        + [in_flight(GOING)] * 4,
        compiler_params=pltpu.CompilerParams(
            collective_id=number, has_side_effects=True, vmem_limit_bytes=50 * 2**20
        ),
        cost_estimate=pl.CostEstimate(flops=2_000_000_000, bytes_accessed=4 * 2**20, transcendentals=4_000_000),
    )(plan.reshape(1, -1), lengths.T, queries, keys, values)


def local(queries, keys, values, lengths, plan):
    queries, keys, values = (array.reshape(CAP, BLOCK, -1) for array in (queries, keys, values))
    forms = [functools.partial(exchange, number, left_out) for number, left_out in enumerate(FORMS)]
    attended = lax.switch(first_form(plan), forms, queries, keys, values, lengths, plan)
    return attended.reshape(CAP * BLOCK, -1)


def solution(mesh):
    placed = (
        P(("seq", "head"), None),
        P(("seq", "head"), None),
        P(("seq", "head"), None),
        P(),
        P(),
    )
    return jax.shard_map(
        local, mesh=mesh, in_specs=placed, out_specs=P(("seq", "head"), None), check_vma=False
    )
```

```python
import functools
import math

import jax
import jax.numpy as jnp
from jax import lax
from jax.experimental import pallas as pl
from jax.experimental.pallas import tpu as pltpu
from jax.sharding import PartitionSpec as P

HEAD_DIM = 128
BLOCK = 128
SEQ = 16
SIDE = 4
HEAD = 8
BPG = 16
CAP = 2
LONGEST = 10
HEADS_HERE = 2
PAD = LONGEST - 1
REACHES = ((0, 4), (4, 8), (8, BPG))
MESH = pl.DeviceIdType.MESH
SCALE = 1.0 / math.sqrt(HEAD_DIM)
LOG2E = 1.4426950408889634
QUERY, KEY, VALUE = 0, 1, 2

COMING = (
    (KEY, 0, 0, 64),
    (KEY, 0, 64, 64),
    (QUERY, 0, 0, 64),
    (QUERY, 0, 64, 64),
    (VALUE, 0, 0, 64),
    (VALUE, 0, 64, 64),
    (KEY, 1, 0, 128),
    (QUERY, 1, 0, 128),
    (VALUE, 1, 0, 64),
    (VALUE, 1, 64, 64),
)
GOING = ((0, 0, 64), (0, 64, 64), (1, 0, 64), (1, 64, 64))
AHEAD = 5

FORMS = (
    (2, 6, 8, 9, 10), (6, 7, 8, 13, 14), (2, 7, 8, 10, 14), (5, 6, 8, 10, 14),
    (3, 6, 8, 9, 14), (3, 6, 8, 10, 13), (2, 6, 8, 10, 11), (6, 8, 14), (),
)


def spots(left_out):
    return tuple(offset for offset in range(1, SEQ) if offset not in left_out)


def first_form(plan):
    offset = (plan // BPG - jnp.arange(plan.shape[0], dtype=jnp.int32) // BPG) % SEQ
    shift = jnp.arange(SEQ, dtype=jnp.int32)
    moved = (offset[None, :] - shift[:, None]) % SEQ
    against = jnp.zeros_like(moved)
    for one in range(1, SEQ):
        against = jnp.where(moved == one, sum(1 << n for n, left_out in enumerate(FORMS) if one in left_out), against)
    against = lax.reduce(against, jnp.int32(0), lax.bitwise_or, (1,))
    form = jnp.full((SEQ,), len(FORMS) - 1, jnp.int32)
    for number in reversed(range(len(FORMS) - 1)):
        form = jnp.where(against & (1 << number) == 0, number, form)
    return jnp.min(form)


def fill_tables(left_out, plan, here, columns):
    cells = CAP * (SEQ - len(left_out))
    wide = (1, SEQ * BPG)
    lane = lax.broadcasted_iota(jnp.int32, wide, 1)
    source, ids = lane // BPG, lane % BPG
    dest, slot = plan[...] // BPG, plan[...] % BPG
    straight = (dest - source) % SEQ
    shift = jnp.zeros((1, 1), jnp.int32)
    if left_out:
        tried = lax.broadcasted_iota(jnp.int32, (SEQ, SEQ * BPG), 0)
        moved = (straight - tried) % SEQ
        misses = functools.reduce(jnp.add, [(moved == one).astype(jnp.int32) for one in left_out])
        misses = jnp.sum(misses, axis=1, keepdims=True)
        rows = lax.broadcasted_iota(jnp.int32, (SEQ, 1), 0)
        shift = jnp.min(jnp.where(misses == 0, rows, SEQ - 1), axis=0, keepdims=True)
    rank = jnp.zeros(wide, jnp.int32)
    for back in range(1, BPG):
        earlier = pltpu.roll(dest, back, 1)
        rank = rank + ((earlier == dest) & (ids >= back)).astype(jnp.int32)
    place = (dest - shift) % SEQ
    offset = (straight - shift) % SEQ
    spot = offset
    for one in left_out:
        spot = spot - (offset > one).astype(jnp.int32)
    cell = spot * CAP + rank
    going, coming = source == here, place == here

    def pick(count, chosen, key, value, limit):
        rows = lax.broadcasted_iota(jnp.int32, (count, SEQ * BPG), 0)
        picked = jnp.sum(jnp.where(chosen & (key == rows), value, 0), axis=1, keepdims=True)
        return jnp.minimum(picked, limit - 1)

    found = jnp.concatenate(
        [
            jnp.pad(pick(cells, going, cell, ids, BPG), ((0, SEQ * CAP - cells), (0, 0))),
            pick(BPG, coming, slot, cell, cells),
            jnp.pad(pick(cells, coming, cell, slot, BPG), ((0, SEQ * CAP - cells), (0, 0))),
            pick(BPG, going, ids, cell, cells),
            jnp.broadcast_to(shift, (BLOCK - SHIFT, 1)),
        ],
        axis=0,
    )
    columns[...] = jnp.broadcast_to(found, (BLOCK, BLOCK)).T[:8]


PACK, PLACE, REPACK, RETURN, SHIFT = 0, 32, 48, 80, 96


def kernel(left_out, plan, lengths, q_in, k_in, v_in, out, *scratch):
    scratch = list(scratch)

    def take(count):
        taken, scratch[:] = scratch[:count], scratch[count:]
        return taken

    zbuf, xbuf, pbuf = (take(len(COMING)) for _ in range(3))
    opack, rbuf, zpack = (take(len(GOING)) for _ in range(3))
    obuf, qg, kg, vg, columns, table, t_sem, all_in, z_send, z_recv, x_send, x_recv, y_send, y_recv, w_send, w_recv = scratch
    inputs = (q_in, k_in, v_in)
    offsets = spots(left_out)
    s = lax.axis_index("seq")
    h = lax.axis_index("head")

    def across(offset):
        return (lax.rem(s + offset, SEQ), h)

    def offset_of(spot):
        offset = spot
        for one in left_out:
            offset = offset + (offset >= one).astype(jnp.int32)
        return offset

    def each(first, last, body, unroll=1):
        def step(i, carry):
            body(i)
            return carry

        lax.fori_loop(first, last, step, 0, unroll=unroll)

    def peer(step):
        return lax.rem(h + step, HEAD)

    barrier = pltpu.get_barrier_semaphore()
    for step in range(1, HEAD):
        pl.semaphore_signal(barrier, inc=1, device_id=(s, peer(step)), device_id_type=MESH)
    row, line = s // SIDE, s % SIDE
    beside = [(row * SIDE + lax.rem(line + step, SIDE), h) for step in range(1, SIDE)]
    above = [(lax.rem(row + step, SIDE) * SIDE + line, h) for step in range(1, SIDE)]
    for device in above + beside:
        pl.semaphore_signal(barrier, inc=1, device_id=device, device_id_type=MESH)
    pl.semaphore_wait(barrier, HEAD - 1 + 2 * (SIDE - 1))
    for device in beside:
        pl.semaphore_signal(all_in, inc=1, device_id=device, device_id_type=MESH)

    def columns_of(device, head):
        return pl.ds(pl.multiple_of((device * HEADS_HERE + head) * HEAD_DIM, HEAD_DIM), HEAD_DIM)

    def wait_for(ref, sem):
        pltpu.make_async_copy(ref, ref, sem).wait()

    def z_start(u):
        tensor, head, row, rows = COMING[u]

        def send(step):
            to = peer(step)
            pltpu.make_async_remote_copy(
                src_ref=inputs[tensor].at[:, pl.ds(row, rows), columns_of(to, head)],
                dst_ref=zbuf[u].at[pl.ds(h * CAP, CAP)],
                send_sem=z_send.at[u],
                recv_sem=z_recv.at[u],
                device_id=(s, to),
                device_id_type=MESH,
            ).start()

        each(1, HEAD, send)
        pltpu.make_async_copy(
            inputs[tensor].at[:, pl.ds(row, rows), columns_of(h, head)], zbuf[u].at[pl.ds(h * CAP, CAP)], z_recv.at[u]
        ).start()

    def z_wait(u):
        wait_for(zbuf[u], z_recv.at[u])

    def x_start(u):
        def send(spot):
            for j in range(CAP):
                pbuf[u][(spot - 1) * CAP + j] = zbuf[u][table[0, PACK + spot * CAP + j]]
            pltpu.make_async_remote_copy(
                src_ref=pbuf[u].at[pl.ds((spot - 1) * CAP, CAP)],
                dst_ref=xbuf[u].at[pl.ds(spot * CAP, CAP)],
                send_sem=x_send.at[u],
                recv_sem=x_recv.at[u],
                device_id=across(offset_of(spot)),
                device_id_type=MESH,
            ).start()

        each(1, len(offsets) + 1, send)
        for j in range(CAP):
            xbuf[u][j] = zbuf[u][table[0, PACK + j]]

    def x_wait(u):
        wait_for(xbuf[u].at[pl.ds(CAP, len(offsets) * CAP)], x_recv.at[u])

    def collect(head):
        def gather(r, carry):
            index = table[0, PLACE + r]
            for u, (tensor, own, row, rows) in enumerate(COMING):
                if own != head:
                    continue
                ahead = 0 if tensor == QUERY else PAD * BLOCK
                at = pl.ds(pl.multiple_of(r * BLOCK + (ahead + row), rows), rows)
                if tensor == VALUE:
                    vg[at, :HEAD_DIM] = xbuf[u][index]
                else:
                    (qg, kg)[tensor][at] = xbuf[u][index]
            return carry

        lax.fori_loop(0, BPG, gather, 0)

    def attend(head):
        group = lax.rem(s + table[0, SHIFT], SEQ)
        first_end = lengths[0, group]
        second_end = first_end + lengths[1, group]
        down = lax.broadcasted_iota(jnp.int32, (BLOCK, BLOCK), 0)
        along = lax.broadcasted_iota(jnp.int32, (BLOCK, BLOCK), 1)
        corner = jnp.where(along <= down, 0.0, -1e30).astype(jnp.float32)

        def record(index):
            return (index >= first_end).astype(jnp.int32) + (index >= second_end).astype(jnp.int32)

        def block(reach, i):
            span = reach * BLOCK
            theirs = lax.broadcasted_iota(jnp.int32, (1, span), 1) // BLOCK + (i - reach + 1)
            seen = (record(theirs) == record(jnp.full_like(theirs, i))) & (theirs >= 0)
            bias = jnp.where(seen, 0.0, -1e30).astype(jnp.float32)
            rows = pl.ds(pl.multiple_of(i * BLOCK, BLOCK), BLOCK)
            window = pl.ds(pl.multiple_of((i + LONGEST - reach) * BLOCK, BLOCK), span)
            scores = lax.dot_general(
                qg[rows], kg[window], (((1,), (1,)), ((), ())), preferred_element_type=jnp.float32
            )
            scores = jnp.concatenate(
                [scores[:, : span - BLOCK] + bias[:, : span - BLOCK], scores[:, span - BLOCK :] + corner], axis=1
            )
            peak = jnp.max(scores, axis=1, keepdims=True)
            weights = jnp.exp2((scores - peak) * (SCALE * LOG2E)).astype(jnp.bfloat16)
            both = jnp.dot(weights, vg[window], preferred_element_type=jnp.float32)
            obuf[head * BPG + i] = (both[:, :HEAD_DIM] / both[:, HEAD_DIM:]).astype(jnp.bfloat16)

        for begin, end in REACHES:
            each(begin, end, functools.partial(block, min(end, LONGEST)), min(end - begin, 4))

    def y_start(w):
        head, row, rows = GOING[w]

        def send(spot):
            for j in range(CAP):
                opack[w][(spot - 1) * CAP + j] = obuf[table[0, REPACK + spot * CAP + j] + head * BPG, row : row + rows]
            pltpu.make_async_remote_copy(
                src_ref=opack[w].at[pl.ds((spot - 1) * CAP, CAP)],
                dst_ref=rbuf[w].at[pl.ds(spot * CAP, CAP)],
                send_sem=y_send.at[w],
                recv_sem=y_recv.at[w],
                device_id=across(SEQ - offset_of(spot)),
                device_id_type=MESH,
            ).start()

        each(1, len(offsets) + 1, send)
        for j in range(CAP):
            rbuf[w][j] = obuf[table[0, REPACK + j] + head * BPG, row : row + rows]

    def w_start(w):
        head, row, rows = GOING[w]
        wait_for(rbuf[w].at[pl.ds(CAP, len(offsets) * CAP)], y_recv.at[w])
        target = out.at[:, pl.ds(row, rows), columns_of(h, head)]

        def pack(to):
            for j in range(CAP):
                zpack[w][to, j] = rbuf[w][table[0, RETURN + to * CAP + j]]

        def send(step):
            to = peer(step)
            pack(to)
            pltpu.make_async_remote_copy(
                src_ref=zpack[w].at[to],
                dst_ref=target,
                send_sem=w_send.at[w],
                recv_sem=w_recv.at[w],
                device_id=(s, to),
                device_id_type=MESH,
            ).start()

        each(1, HEAD, send)
        pack(h)
        pltpu.make_async_copy(zpack[w].at[h], target, w_recv.at[w]).start()

    for u in range(AHEAD):
        z_start(u)
    fill_tables(left_out, plan, s, columns)
    fetch = pltpu.make_async_copy(columns, table, t_sem)
    fetch.start()
    kg[: PAD * BLOCK] = jnp.zeros((PAD * BLOCK, HEAD_DIM), jnp.bfloat16)
    vg[: PAD * BLOCK, :HEAD_DIM] = jnp.zeros((PAD * BLOCK, HEAD_DIM), jnp.bfloat16)
    vg[:, HEAD_DIM:] = jnp.ones(((PAD + BPG) * BLOCK, HEAD_DIM), jnp.bfloat16)
    fetch.wait()
    pl.semaphore_wait(all_in, SIDE - 1)
    for u in range(len(COMING)):
        z_wait(u)
        x_start(u)
        if u + AHEAD < len(COMING):
            z_start(u + AHEAD)
    first = [u for u, unit in enumerate(COMING) if unit[1] == 0]
    second = [u for u, unit in enumerate(COMING) if unit[1] == 1]

    def one_head(head):
        @pl.when(head == 0)
        def _():
            for u in first:
                x_wait(u)
            collect(0)

        @pl.when(head == 1)
        def _():
            for u in second[:-1]:
                x_wait(u)
            y_start(0)
            x_wait(second[-1])
            y_start(1)
            collect(1)

        attend(head)

    each(0, HEADS_HERE, one_head)
    y_start(2)
    y_start(3)
    for w in range(len(GOING)):
        w_start(w)
    for u in range(len(COMING)):
        wait_for(zbuf[u].at[pl.ds(0, (HEAD - 1) * CAP)], z_send.at[u])
        wait_for(pbuf[u], x_send.at[u])
    for w, (_, row, rows) in enumerate(GOING):
        wait_for(opack[w], y_send.at[w])
        wait_for(zpack[w].at[pl.ds(0, HEAD - 1)], w_send.at[w])
        wait_for(out.at[:, pl.ds(row, rows), pl.ds(0, HEAD * HEAD_DIM)], w_recv.at[w])


def exchange(number, left_out, queries, keys, values, lengths, plan):
    bf16 = jnp.bfloat16
    count = len(spots(left_out))

    def blocks(many, rows):
        return pltpu.VMEM((many, rows, HEAD_DIM), bf16)

    def in_flight(units):
        return pltpu.SemaphoreType.DMA((len(units),))

    return pl.pallas_call(
        functools.partial(kernel, left_out),
        out_shape=jax.ShapeDtypeStruct(queries.shape, bf16),
        in_specs=[pl.BlockSpec(memory_space=pltpu.VMEM), pl.BlockSpec(memory_space=pltpu.SMEM)]
        + [pl.BlockSpec(memory_space=pl.ANY)] * 3,
        out_specs=pl.BlockSpec(memory_space=pl.ANY),
        scratch_shapes=[blocks(BPG, unit[3]) for unit in COMING]
        + [blocks((count + 1) * CAP, unit[3]) for unit in COMING]
        + [blocks(count * CAP, unit[3]) for unit in COMING]
        + [blocks(count * CAP, unit[2]) for unit in GOING]
        + [blocks((count + 1) * CAP, unit[2]) for unit in GOING]
        + [pltpu.VMEM((HEAD, CAP, unit[2], HEAD_DIM), bf16) for unit in GOING]
        + [
            blocks(HEADS_HERE * BPG, BLOCK),
            pltpu.VMEM((BPG * BLOCK, HEAD_DIM), bf16),
            pltpu.VMEM(((PAD + BPG) * BLOCK, HEAD_DIM), bf16),
            pltpu.VMEM(((PAD + BPG) * BLOCK, 2 * HEAD_DIM), bf16),
            pltpu.VMEM((8, BLOCK), jnp.int32),
            pltpu.SMEM((8, BLOCK), jnp.int32),
            pltpu.SemaphoreType.DMA,
            pltpu.SemaphoreType.REGULAR,
        ]
        + [in_flight(COMING)] * 4
        + [in_flight(GOING)] * 4,
        compiler_params=pltpu.CompilerParams(
            collective_id=number, has_side_effects=True, vmem_limit_bytes=50 * 2**20
        ),
        cost_estimate=pl.CostEstimate(flops=2_000_000_000, bytes_accessed=4 * 2**20, transcendentals=4_000_000),
    )(plan.reshape(1, -1), lengths.T, queries, keys, values)


def local(queries, keys, values, lengths, plan):
    queries, keys, values = (array.reshape(CAP, BLOCK, -1) for array in (queries, keys, values))
    forms = [functools.partial(exchange, number, left_out) for number, left_out in enumerate(FORMS)]
    attended = lax.switch(first_form(plan), forms, queries, keys, values, lengths, plan)
    return attended.reshape(CAP * BLOCK, -1)


def solution(mesh):
    placed = (
        P(("seq", "head"), None),
        P(("seq", "head"), None),
        P(("seq", "head"), None),
        P(),
        P(),
    )
    return jax.shard_map(
        local, mesh=mesh, in_specs=placed, out_specs=P(("seq", "head"), None), check_vma=False
    )
```
